32 devices in a mesh: wide: 8 (over y, x, core), blk: 4 (over z).
Axes of the slice: x: 2, y: 2, z: 4, core: 2. Of those that a mesh axis runs over, the one named last changes fastest.
Arguments:
- features: bfloat16 [512, 768], P('blk'), may hold values from -6 to 6
- weights: bfloat16 [32768, 768], P(('wide', 'blk')), may hold values from -0.21875 to 0.21875
- momentum: bfloat16 [32768, 768], P(('wide', 'blk')), may hold values from -48 to 48
- targets: bfloat16 [512, 32768], P(None, ('wide', 'blk')), may hold values from 0 to 1
Outputs:
- new_weights: bfloat16 [32768, 768], P(('wide', 'blk'))
- new_momentum: bfloat16 [32768, 768], P(('wide', 'blk'))
- feature_grad: bfloat16 [512, 768], P('blk', 'wide')
The draws below stay inside these ranges and needn't reach their ends.
All inputs are finite; a program needn't handle non-finite values.
Results may differ from the reference program's by a relative error of at most 0.009.
Values may be sent and summed in bfloat16 or wider, within the bound.
A program may use at most 64 MiB of HBM per device.

```python
import math
import jax
import jax.numpy as jnp
from jax import lax

D = 768
LABELS = 32768
ROWS = 512


def block_scale(rng, shape, split, low, largest):
    def one(axis_at, blocks):
        draws = jax.random.uniform(jax.random.fold_in(jax.random.fold_in(rng, 6), axis_at), (blocks,), jnp.float32, low / len(split), largest / len(split))
        return jnp.repeat(jnp.exp(draws), shape[axis_at] // blocks).reshape((-1,) + (1,) * (len(shape) - axis_at - 1))

    factor_of = one(*split[0])
    for cut in split[1:]:
        factor_of = factor_of * one(*cut)
    return factor_of


def gaussian(rng, extent, scale, bound, cuts=(), held_as=jnp.bfloat16):
    values = scale * jax.random.normal(rng, extent, jnp.float32)
    if cuts:
        values = values * block_scale(rng, extent, cuts, -0.22, 0.18)
    return jnp.clip(values, -bound, bound).astype(held_as)


def setup_inputs(seed: int = 0) -> dict:
    keys = jax.random.split(jax.random.key(seed), 5)
    features = gaussian(keys[0], (ROWS, D), 1.0, 6.0, ((0, 4),))
    weights = gaussian(keys[1], (LABELS, D), D ** -0.5, 0.21875, ((0, 32),))
    momentum = gaussian(keys[2], (LABELS, D), 8.0, 48.0, ((0, 32),))
    targets = jnp.clip(1.0 * jax.random.uniform(keys[3], (ROWS, LABELS), jnp.float32) ** block_scale(keys[3], (ROWS, LABELS), ((1, 32),), -0.2, 0.2), 0.0, 1.0).astype(jnp.bfloat16)
    return dict(features=features, weights=weights, momentum=momentum, targets=targets)


def reference(features, weights, momentum, targets):
    width = math.gcd(LABELS, 8192)
    nblocks = LABELS // width

    def one_block(totals, index):
        start = (index * width).astype(jnp.int32)
        weight_rows = lax.dynamic_slice_in_dim(weights, start, width, 0)
        moment_rows = lax.dynamic_slice_in_dim(momentum, start, width, 0)
        target_cols = lax.dynamic_slice_in_dim(targets, start, width, 1)
        scores = jnp.dot(features, weight_rows.T, preferred_element_type=jnp.float32)
        errors = (jax.nn.sigmoid(scores) - target_cols.astype(jnp.float32)).astype(jnp.bfloat16)
        grad = jnp.dot(errors.T, features, preferred_element_type=jnp.float32)
        moment_new = (0.9 * moment_rows.astype(jnp.float32) + grad).astype(jnp.bfloat16)
        weight_new = (weight_rows.astype(jnp.float32) - 0.002 * moment_new.astype(jnp.float32)).astype(jnp.bfloat16)
        totals = totals + jnp.dot(errors, weight_rows, preferred_element_type=jnp.float32)
        return totals, (weight_new, moment_new)

    totals, (weight_all, moment_all) = lax.scan(one_block, jnp.zeros((ROWS, D), jnp.float32), jnp.arange(nblocks, dtype=jnp.int32))
    return weight_all.reshape(LABELS, D), moment_all.reshape(LABELS, D), totals.astype(jnp.bfloat16)
```

```python
import functools

import jax
import jax.numpy as jnp
from jax import lax
from jax.experimental import pallas as pl
from jax.experimental.pallas import tpu as pltpu
from jax.sharding import PartitionSpec as P

F32 = jnp.float32
BF16 = jnp.bfloat16
MESH = pl.DeviceIdType.MESH


def mult(value, by):
    return value if isinstance(value, int) else pl.multiple_of(value, by)


def kernel(
    nw, nb, split,
    feat_ref, w_hbm, m_hbm, t_hbm,
    ow_hbm, om_hbm, fg_ref,
    feat, w_v, m_v, t_v, tt, wt, err,
    a_send, a_recv, part, b_send, b_recv, c_send, c_own, c_recv, ow_v, om_v,
    load_sem, store_sem, zs, zr, ps, pr, cs, cr, as_, ar, bs, br, xs, xr,
):
    rows = feat_ref.shape[0]
    labels, width = w_hbm.shape
    chips = nw // 2
    bw = width // nw
    pairs = nb // 2
    half = rows // 2
    piece = half // split

    wide = lax.axis_index("wide")
    blk = lax.axis_index("blk")
    core = lax.rem(wide, 2)
    chip = lax.div(wide, 2)
    mate_core = 1 - core
    partner = chip * 2 + mate_core
    slot = lax.rem(chip, split)
    group = chip - slot
    pair = lax.div(blk, 2)
    mate = pair * 2 + 1 - lax.rem(blk, 2)

    def pair_at(i):
        return lax.rem(pair + i, pairs)

    sources = [mate]
    for i in range(1, pairs):
        sources += [pair_at(i) * 2, pair_at(i) * 2 + 1]
    targets_z = [mate]
    for i in range(1, pairs):
        back = lax.rem(pair - i + pairs, pairs)
        targets_z += [back * 2, back * 2 + 1]

    def feat_at(block, first, count):
        start = lax.rem(block, 2) * rows + first
        return feat.at[lax.div(block, 2), pl.ds(mult(start, 16), count)]

    loads = [
        pltpu.make_async_copy(feat_ref, feat_at(blk, 0, rows), load_sem.at[0]),
        pltpu.make_async_copy(w_hbm, w_v, load_sem.at[1]),
        pltpu.make_async_copy(t_hbm, t_v, load_sem.at[2]),
        pltpu.make_async_copy(m_hbm, m_v, load_sem.at[3]),
    ]
    for load in loads:
        load.start()

    barrier = pltpu.get_barrier_semaphore()
    peers = [(partner, blk)]
    peers += [(lax.rem(chip + d, chips) * 2 + core, blk) for d in range(1, chips)]
    peers += [(wide, lax.rem(blk + d, nb)) for d in range(1, nb)]
    for peer in peers:
        pl.semaphore_signal(barrier, inc=1, device_id=peer, device_id_type=MESH)
    pl.semaphore_wait(barrier, len(peers))

    def remote(src, dst, send, recv, peer):
        return pltpu.make_async_remote_copy(
            src_ref=src, dst_ref=dst, send_sem=send, recv_sem=recv,
            device_id=peer, device_id_type=MESH,
        )

    sent = []
    mine = core * half + slot * piece

    for target in targets_z:
        copy = remote(
            feat_ref.at[pl.ds(mult(mine, 16), piece)], feat_at(blk, mine, piece),
            zs.at[target], zr.at[blk], (wide, target),
        )
        copy.start()
        sent.append(copy)

    def spread(source):
        here = feat_at(source, mine, piece)
        remote(here, here, zs.at[source], zr.at[source], (wide, source)).wait_recv()
        for d in range(1, split):
            other = lax.rem(slot + d, split)
            copy = remote(
                here, here, ps.at[source, other], pr.at[source, slot],
                ((group + other) * 2 + core, blk),
            )
            copy.start()
            sent.append(copy)

    def cross(source):
        for d in range(1, split):
            other = lax.rem(slot + d, split)
            there = feat_at(source, core * half + other * piece, piece)
            remote(
                there, there, ps.at[source, other], pr.at[source, other],
                ((group + other) * 2 + core, blk),
            ).wait_recv()
        lot = feat_at(source, core * half, half)
        copy = remote(lot, lot, cs.at[source], cr.at[source], (partner, blk))
        copy.start()
        sent.append(copy)

    def arrived(source):
        lot = feat_at(source, mate_core * half, half)
        remote(lot, lot, cs.at[source], cr.at[source], (partner, blk)).wait_recv()

    def turn_weights(first, last):
        for c in range(first, last):
            turned = w_v[:, 128 * c:128 * (c + 1)].T
            at = 128 * c
            while at < 128 * (c + 1):
                block, off = at // bw, at % bw
                count = min(bw - off, 128 * (c + 1) - at)
                to = (block // 2) * bw + off
                wt[block % 2, to:to + count, :] = turned[at - 128 * c:at - 128 * c + count]
                at += count

    def turn_targets(i):
        p = pair_at(i)
        first = mult(p * 2 * rows, 2 * rows)
        tt[p] = t_v[pl.ds(first, 2 * rows), :].T

    tiles = width // 128
    loads[1].wait()
    turn_weights(0, tiles // 2)
    spread(sources[0])
    turn_weights(tiles // 2, tiles)
    for source in sources[1:]:
        spread(source)
    cross(sources[0])
    loads[2].wait()
    turn_targets(0)
    for source in sources[1:]:
        cross(source)
    for i in range(1, pairs):
        turn_targets(i)
    loads[0].wait()

    step = min(512, labels)

    def errors(i):
        p = pair_at(i)
        for first in range(0, labels, step):
            scores = lax.dot_general(
                w_v[first:first + step], feat[p], (((1,), (1,)), ((), ())),
                preferred_element_type=F32,
            )
            chance = 0.5 * jnp.tanh(0.5 * scores) + 0.5
            err[p, first:first + step] = (
                chance - tt[p, first:first + step].astype(F32)
            ).astype(BF16)

    def back(p, which):
        return jnp.dot(wt[which], err[p], preferred_element_type=F32)

    def pair_copy(p):
        return remote(a_send.at[p], a_recv.at[p], as_.at[p], ar.at[p], (partner, blk))

    def first_half(i):
        p = pair_at(i)
        a_send[p] = back(p, mate_core).astype(BF16)
        copy = pair_copy(p)
        copy.start()
        sent.append(copy)

    def second_half(i):
        p = pair_at(i)
        part[p] = back(p, core).reshape(chips, bw, 2 * rows)

    def to_chips(i):
        p = pair_at(i)
        pair_copy(p).wait_recv()
        total = part[p] + a_recv[p].astype(F32).reshape(chips, bw, 2 * rows)
        part[p] = total
        b_send[p] = total.astype(BF16)
        for d in range(1, chips):
            other = lax.rem(chip + d, chips)
            copy = remote(
                b_send.at[p, other], b_recv.at[p, chip], bs.at[p, other], br.at[p, chip],
                (other * 2 + core, blk),
            )
            copy.start()
            sent.append(copy)

    def to_blocks(i):
        p = pair_at(i)
        total = part[p, chip]
        for d in range(1, chips):
            other = lax.rem(chip + d, chips)
            remote(
                b_send.at[p, other], b_recv.at[p, other], bs.at[p, other], br.at[p, other],
                (other * 2 + core, blk),
            ).wait_recv()
            total = total + b_recv[p, other].astype(F32)
        for n in range(2):
            c_own[p * 2 + n] = total[:, n * rows:(n + 1) * rows]
            c_send[p * 2 + n] = total[:, n * rows:(n + 1) * rows].astype(BF16)
        for target in [mate] if i == 0 else [p * 2, p * 2 + 1]:
            copy = remote(
                c_send.at[target], c_recv.at[blk], xs.at[target], xr.at[blk], (wide, target)
            )
            copy.start()
            sent.append(copy)

    stores = []
    chunk = min(256, labels)

    def update(n):
        first = n * chunk
        span = slice(first, first + chunk)
        grad = jnp.dot(err[0, span], feat[0], preferred_element_type=F32)
        for p in range(1, pairs):
            grad = grad + jnp.dot(err[p, span], feat[p], preferred_element_type=F32)
        moment = (0.9 * m_v[span].astype(F32) + grad).astype(BF16)
        om_v[span] = moment
        ow_v[span] = (w_v[span].astype(F32) - 0.002 * moment.astype(F32)).astype(BF16)
        for k, (src, dst) in enumerate(((om_v, om_hbm), (ow_v, ow_hbm))):
            copy = pltpu.make_async_copy(
                src.at[pl.ds(first, chunk)], dst.at[pl.ds(first, chunk)], store_sem.at[k, n]
            )
            copy.start()
            stores.append(copy)

    updates = list(range(labels // chunk))

    def some_updates(count):
        for n in updates[:count]:
            update(n)
        del updates[:count]

    arrived(sources[0])
    errors(0)
    first_half(0)
    second_half(0)
    for i in range(1, pairs):
        arrived(sources[2 * i - 1])
        arrived(sources[2 * i])
        errors(i)
        first_half(i)
        to_chips(i - 1)
        second_half(i)
        if i >= 2:
            to_blocks(i - 2)
    to_chips(pairs - 1)
    loads[3].wait()
    some_updates(1)
    if pairs >= 2:
        to_blocks(pairs - 2)
    some_updates(2)
    to_blocks(pairs - 1)
    some_updates(len(updates))

    total = c_own[blk]
    for d in range(1, nb):
        other = lax.rem(blk + d, nb)
        remote(
            c_send.at[other], c_recv.at[other], xs.at[other], xr.at[other], (wide, other)
        ).wait_recv()
        total = total + c_recv[other].astype(F32)
    fg_ref[...] = total.T.astype(BF16)

    for copy in sent:
        copy.wait_send()
    for copy in stores:
        copy.wait()


def solution(mesh):
    nw, nb = mesh.shape["wide"], mesh.shape["blk"]
    chips = nw // 2

    def shards(features, weights, momentum, targets):
        rows, width = features.shape
        labels = weights.shape[0]
        split = chips
        while split > 1 and (chips % split or rows % (32 * split)):
            split -= 1
        bw = width // nw
        pairs = nb // 2
        total_rows = targets.shape[0]
        flops = 6 * total_rows * labels * width
        hbm = pl.BlockSpec(memory_space=pl.ANY)
        vmem = pl.BlockSpec(memory_space=pltpu.VMEM)
        dma = pltpu.SemaphoreType.DMA
        chunks = labels // min(256, labels)
        new_weights, new_momentum, feature_grad = pl.pallas_call(
            functools.partial(kernel, nw, nb, split),
            out_shape=(
                jax.ShapeDtypeStruct(weights.shape, BF16),
                jax.ShapeDtypeStruct(momentum.shape, BF16),
                jax.ShapeDtypeStruct((rows, bw), BF16),
            ),
            in_specs=[hbm, hbm, hbm, hbm],
            out_specs=(hbm, hbm, vmem),
            scratch_shapes=[
                pltpu.VMEM((pairs, 2 * rows, width), BF16),
                pltpu.VMEM((labels, width), BF16),
                pltpu.VMEM((labels, width), BF16),
                pltpu.VMEM((total_rows, labels), BF16),
                pltpu.VMEM((pairs, labels, 2 * rows), BF16),
                pltpu.VMEM((2, width // 2, labels), BF16),
                pltpu.VMEM((pairs, labels, 2 * rows), BF16),
                pltpu.VMEM((pairs, width // 2, 2 * rows), BF16),
                pltpu.VMEM((pairs, width // 2, 2 * rows), BF16),
                pltpu.VMEM((pairs, chips, bw, 2 * rows), F32),
                pltpu.VMEM((pairs, chips, bw, 2 * rows), BF16),
                pltpu.VMEM((pairs, chips, bw, 2 * rows), BF16),
                pltpu.VMEM((nb, bw, rows), BF16),
                pltpu.VMEM((nb, bw, rows), F32),
                pltpu.VMEM((nb, bw, rows), BF16),
                pltpu.VMEM((labels, width), BF16),
                pltpu.VMEM((labels, width), BF16),
                dma((4,)), dma((2, chunks)),
                dma((nb,)), dma((nb,)),
                dma((nb, split)), dma((nb, split)),
                dma((nb,)), dma((nb,)),
                dma((pairs,)), dma((pairs,)),
                dma((pairs, chips)), dma((pairs, chips)),
                dma((nb,)), dma((nb,)),
            ],
            compiler_params=pltpu.CompilerParams(
                collective_id=0, has_side_effects=True, vmem_limit_bytes=56 * 1024 * 1024
            ),
            cost_estimate=pl.CostEstimate(
                flops=flops, bytes_accessed=8 * labels * width, transcendentals=total_rows * labels
            ),
        )(features, weights, momentum, targets)
        return new_weights, new_momentum, feature_grad

    placed = (
        P("blk", None),
        P(("wide", "blk"), None),
        P(("wide", "blk"), None),
        P(None, ("wide", "blk")),
    )
    return jax.shard_map(
        shards,
        mesh=mesh,
        in_specs=placed,
        out_specs=(P(("wide", "blk"), None), P(("wide", "blk"), None), P("blk", "wide")),
        check_vma=False,
    )
```

```python
import functools

import jax
import jax.numpy as jnp
from jax import lax
from jax.experimental import pallas as pl
from jax.experimental.pallas import tpu as pltpu
from jax.sharding import PartitionSpec as P

F32 = jnp.float32
BF16 = jnp.bfloat16
MESH = pl.DeviceIdType.MESH


def mult(value, by):
    return value if isinstance(value, int) else pl.multiple_of(value, by)


def kernel(
    nw, nb, split,
    feat_ref, w_hbm, m_hbm, t_hbm,
    ow_v, om_v, fg_ref,
    feat, w_v, m_v, t_v, tt, wt, err,
    a_send, a_recv, part, b_send, b_recv, c_send, c_own, c_recv,
    load_sem, zs, zr, ps, pr, cs, cr, as_, ar, bs, br, xs, xr,
):
    rows = feat_ref.shape[0]
    labels, width = w_hbm.shape
    chips = nw // 2
    bw = width // nw
    pairs = nb // 2
    half = rows // 2
    piece = half // split

    wide = lax.axis_index("wide")
    blk = lax.axis_index("blk")
    core = lax.rem(wide, 2)
    chip = lax.div(wide, 2)
    mate_core = 1 - core
    partner = chip * 2 + mate_core
    slot = lax.rem(chip, split)
    group = chip - slot
    pair = lax.div(blk, 2)
    mate = pair * 2 + 1 - lax.rem(blk, 2)

    def pair_at(i):
        return lax.rem(pair + i, pairs)

    sources = [mate]
    for i in range(1, pairs):
        sources += [pair_at(i) * 2, pair_at(i) * 2 + 1]
    targets_z = [mate]
    for i in range(1, pairs):
        back = lax.rem(pair - i + pairs, pairs)
        targets_z += [back * 2, back * 2 + 1]

    def feat_at(block, first, count):
        start = lax.rem(block, 2) * rows + first
        return feat.at[lax.div(block, 2), pl.ds(mult(start, 16), count)]

    loads = [
        pltpu.make_async_copy(feat_ref, feat_at(blk, 0, rows), load_sem.at[0]),
        pltpu.make_async_copy(w_hbm, w_v, load_sem.at[1]),
        pltpu.make_async_copy(t_hbm, t_v, load_sem.at[2]),
        pltpu.make_async_copy(m_hbm, m_v, load_sem.at[3]),
    ]
    for load in loads:
        load.start()

    barrier = pltpu.get_barrier_semaphore()
    peers = [(partner, blk)]
    peers += [(lax.rem(chip + d, chips) * 2 + core, blk) for d in range(1, chips)]
    peers += [(wide, lax.rem(blk + d, nb)) for d in range(1, nb)]
    for peer in peers:
        pl.semaphore_signal(barrier, inc=1, device_id=peer, device_id_type=MESH)
    pl.semaphore_wait(barrier, len(peers))

    def remote(src, dst, send, recv, peer):
        return pltpu.make_async_remote_copy(
            src_ref=src, dst_ref=dst, send_sem=send, recv_sem=recv,
            device_id=peer, device_id_type=MESH,
        )

    sent = []
    mine = core * half + slot * piece

    for target in targets_z:
        copy = remote(
            feat_ref.at[pl.ds(mult(mine, 16), piece)], feat_at(blk, mine, piece),
            zs.at[target], zr.at[blk], (wide, target),
        )
        copy.start()
        sent.append(copy)

    def spread(source):
        here = feat_at(source, mine, piece)
        remote(here, here, zs.at[source], zr.at[source], (wide, source)).wait_recv()
        for d in range(1, split):
            other = lax.rem(slot + d, split)
            copy = remote(
                here, here, ps.at[source, other], pr.at[source, slot],
                ((group + other) * 2 + core, blk),
            )
            copy.start()
            sent.append(copy)

    def cross(source):
        for d in range(1, split):
            other = lax.rem(slot + d, split)
            there = feat_at(source, core * half + other * piece, piece)
            remote(
                there, there, ps.at[source, other], pr.at[source, other],
                ((group + other) * 2 + core, blk),
            ).wait_recv()
        lot = feat_at(source, core * half, half)
        copy = remote(lot, lot, cs.at[source], cr.at[source], (partner, blk))
        copy.start()
        sent.append(copy)

    def arrived(source):
        lot = feat_at(source, mate_core * half, half)
        remote(lot, lot, cs.at[source], cr.at[source], (partner, blk)).wait_recv()

    def turn_weights(first, last):
        for c in range(first, last):
            turned = w_v[:, 128 * c:128 * (c + 1)].T
            at = 128 * c
            while at < 128 * (c + 1):
                block, off = at // bw, at % bw
                count = min(bw - off, 128 * (c + 1) - at)
                to = (block // 2) * bw + off
                wt[block % 2, to:to + count, :] = turned[at - 128 * c:at - 128 * c + count]
                at += count

    def turn_targets(i):
        p = pair_at(i)
        first = mult(p * 2 * rows, 2 * rows)
        tt[p] = t_v[pl.ds(first, 2 * rows), :].T

    tiles = width // 128
    loads[1].wait()
    turn_weights(0, tiles // 3)
    spread(sources[0])
    turn_weights(tiles // 3, tiles // 2)
    for source in sources[1:]:
        spread(source)
    cross(sources[0])
    turn_weights(tiles // 2, tiles)
    for source in sources[1:]:
        cross(source)
    loads[2].wait()
    for i in range(pairs):
        turn_targets(i)
    loads[0].wait()

    step = min(512, labels)

    def errors(i):
        p = pair_at(i)
        for first in range(0, labels, step):
            scores = lax.dot_general(
                w_v[first:first + step], feat[p], (((1,), (1,)), ((), ())),
                preferred_element_type=F32,
            )
            chance = 0.5 * jnp.tanh(0.5 * scores) + 0.5
            err[p, first:first + step] = (
                chance - tt[p, first:first + step].astype(F32)
            ).astype(BF16)

    def back(p, which):
        return jnp.dot(wt[which], err[p], preferred_element_type=F32)

    def pair_copy(p):
        return remote(a_send.at[p], a_recv.at[p], as_.at[p], ar.at[p], (partner, blk))

    def first_half(i):
        p = pair_at(i)
        a_send[p] = back(p, mate_core).astype(BF16)
        copy = pair_copy(p)
        copy.start()
        sent.append(copy)

    def second_half(i):
        p = pair_at(i)
        part[p] = back(p, core).reshape(chips, bw, 2 * rows)

    def to_chips(i):
        p = pair_at(i)
        pair_copy(p).wait_recv()
        total = part[p] + a_recv[p].astype(F32).reshape(chips, bw, 2 * rows)
        part[p] = total
        b_send[p] = total.astype(BF16)
        for d in range(1, chips):
            other = lax.rem(chip + d, chips)
            copy = remote(
                b_send.at[p, other], b_recv.at[p, chip], bs.at[p, other], br.at[p, chip],
                (other * 2 + core, blk),
            )
            copy.start()
            sent.append(copy)

    def to_blocks(i):
        p = pair_at(i)
        total = part[p, chip]
        for d in range(1, chips):
            other = lax.rem(chip + d, chips)
            remote(
                b_send.at[p, other], b_recv.at[p, other], bs.at[p, other], br.at[p, other],
                (other * 2 + core, blk),
            ).wait_recv()
            total = total + b_recv[p, other].astype(F32)
        for n in range(2):
            c_own[p * 2 + n] = total[:, n * rows:(n + 1) * rows]
            c_send[p * 2 + n] = total[:, n * rows:(n + 1) * rows].astype(BF16)
        for target in [mate] if i == 0 else [p * 2, p * 2 + 1]:
            copy = remote(
                c_send.at[target], c_recv.at[blk], xs.at[target], xr.at[blk], (wide, target)
            )
            copy.start()
            sent.append(copy)

    chunk = min(256, labels)

    def update(n):
        first = n * chunk
        span = slice(first, first + chunk)
        grad = jnp.dot(err[0, span], feat[0], preferred_element_type=F32)
        for p in range(1, pairs):
            grad = grad + jnp.dot(err[p, span], feat[p], preferred_element_type=F32)
        moment = (0.9 * m_v[span].astype(F32) + grad).astype(BF16)
        om_v[span] = moment
        ow_v[span] = (w_v[span].astype(F32) - 0.002 * moment.astype(F32)).astype(BF16)

    updates = list(range(labels // chunk))

    def some_updates(count):
        for n in updates[:count]:
            update(n)
        del updates[:count]

    arrived(sources[0])
    errors(0)
    first_half(0)
    second_half(0)
    for i in range(1, pairs):
        arrived(sources[2 * i - 1])
        arrived(sources[2 * i])
        errors(i)
        first_half(i)
        to_chips(i - 1)
        second_half(i)
        if i >= 2:
            to_blocks(i - 2)
    to_chips(pairs - 1)
    loads[3].wait()
    some_updates(1)
    if pairs >= 2:
        to_blocks(pairs - 2)
    some_updates(2)
    to_blocks(pairs - 1)
    some_updates(len(updates))

    total = c_own[blk]
    for d in range(1, nb):
        other = lax.rem(blk + d, nb)
        remote(
            c_send.at[other], c_recv.at[other], xs.at[other], xr.at[other], (wide, other)
        ).wait_recv()
        total = total + c_recv[other].astype(F32)
    fg_ref[...] = total.astype(BF16)

    for copy in sent:
        copy.wait_send()


def solution(mesh):
    nw, nb = mesh.shape["wide"], mesh.shape["blk"]
    chips = nw // 2

    def shards(features, weights, momentum, targets):
        rows, width = features.shape
        labels = weights.shape[0]
        split = chips
        while split > 1 and (chips % split or rows % (32 * split)):
            split -= 1
        bw = width // nw
        pairs = nb // 2
        total_rows = targets.shape[0]
        flops = 6 * total_rows * labels * width
        hbm = pl.BlockSpec(memory_space=pl.ANY)
        vmem = pl.BlockSpec(memory_space=pltpu.VMEM)
        dma = pltpu.SemaphoreType.DMA
        new_weights, new_momentum, feature_grad = pl.pallas_call(
            functools.partial(kernel, nw, nb, split),
            out_shape=(
                pltpu.VMEM(weights.shape, BF16),
                pltpu.VMEM(momentum.shape, BF16),
                pltpu.VMEM((bw, rows), BF16),
            ),
            in_specs=[hbm, hbm, hbm, hbm],
            out_specs=(vmem, vmem, vmem),
            scratch_shapes=[
                pltpu.VMEM((pairs, 2 * rows, width), BF16),
                pltpu.VMEM((labels, width), BF16),
                pltpu.VMEM((labels, width), BF16),
                pltpu.VMEM((total_rows, labels), BF16),
                pltpu.VMEM((pairs, labels, 2 * rows), BF16),
                pltpu.VMEM((2, width // 2, labels), BF16),
                pltpu.VMEM((pairs, labels, 2 * rows), BF16),
                pltpu.VMEM((pairs, width // 2, 2 * rows), BF16),
                pltpu.VMEM((pairs, width // 2, 2 * rows), BF16),
                pltpu.VMEM((pairs, chips, bw, 2 * rows), F32),
                pltpu.VMEM((pairs, chips, bw, 2 * rows), BF16),
                pltpu.VMEM((pairs, chips, bw, 2 * rows), BF16),
                pltpu.VMEM((nb, bw, rows), BF16),
                pltpu.VMEM((nb, bw, rows), F32),
                pltpu.VMEM((nb, bw, rows), BF16),
                dma((4,)),
                dma((nb,)), dma((nb,)),
                dma((nb, split)), dma((nb, split)),
                dma((nb,)), dma((nb,)),
                dma((pairs,)), dma((pairs,)),
                dma((pairs, chips)), dma((pairs, chips)),
                dma((nb,)), dma((nb,)),
            ],
            compiler_params=pltpu.CompilerParams(
                collective_id=0, has_side_effects=True, vmem_limit_bytes=56 * 1024 * 1024
            ),
            cost_estimate=pl.CostEstimate(
                flops=flops, bytes_accessed=8 * labels * width, transcendentals=total_rows * labels
            ),
        )(features, weights, momentum, targets)
        return new_weights, new_momentum, feature_grad.T

    placed = (
        P("blk", None),
        P(("wide", "blk"), None),
        P(("wide", "blk"), None),
        P(None, ("wide", "blk")),
    )
    return jax.shard_map(
        shards,
        mesh=mesh,
        in_specs=placed,
        out_specs=(P(("wide", "blk"), None), P(("wide", "blk"), None), P("blk", "wide")),
        check_vma=False,
    )
```

```python
import functools

import jax
import jax.numpy as jnp
from jax import lax
from jax.experimental import pallas as pl
from jax.experimental.pallas import tpu as pltpu
from jax.sharding import PartitionSpec as P

F32 = jnp.float32
BF16 = jnp.bfloat16
MESH = pl.DeviceIdType.MESH
parts = 4


def mult(value, by):
    return value if isinstance(value, int) else pl.multiple_of(value, by)


def kernel(
    nw, nb, split,
    feat_ref, w_hbm, m_hbm, t_hbm,
    ow_v, om_v, fg_ref,
    feat, w_v, m_v, t_v, tt, wt, err,
    a_send, a_recv, part, b_send, b_recv, c_send, c_recv,
    load_sem, zs, zr, ps, pr, cs, cr, as_, ar, bs, br, xs, xr,
):
    rows = feat_ref.shape[0]
    labels, width = w_hbm.shape
    chips = nw // 2
    bw = width // nw
    pairs = nb // 2
    half = rows // 2
    piece = half // split

    wide = lax.axis_index("wide")
    blk = lax.axis_index("blk")
    core = lax.rem(wide, 2)
    chip = lax.div(wide, 2)
    mate_core = 1 - core
    partner = chip * 2 + mate_core
    slot = lax.rem(chip, split)
    group = chip - slot
    pair = lax.div(blk, 2)
    mate = pair * 2 + 1 - lax.rem(blk, 2)

    def pair_at(i):
        return lax.rem(pair + i, pairs)

    sources = [mate]
    for i in range(1, pairs):
        sources += [pair_at(i) * 2, pair_at(i) * 2 + 1]
    targets_z = [mate]
    for i in range(1, pairs):
        back = lax.rem(pair - i + pairs, pairs)
        targets_z += [back * 2, back * 2 + 1]

    def feat_at(block, first, count):
        start = lax.rem(block, 2) * rows + first
        return feat.at[lax.div(block, 2), pl.ds(mult(start, 16), count)]

    loads = [
        pltpu.make_async_copy(feat_ref, feat_at(blk, 0, rows), load_sem.at[0]),
        pltpu.make_async_copy(w_hbm, w_v, load_sem.at[1]),
        pltpu.make_async_copy(t_hbm, t_v, load_sem.at[2]),
        pltpu.make_async_copy(m_hbm, m_v, load_sem.at[3]),
    ]
    for load in loads:
        load.start()

    barrier = pltpu.get_barrier_semaphore()
    peers = [(partner, blk)]
    peers += [(lax.rem(chip + d, chips) * 2 + core, blk) for d in range(1, chips)]
    peers += [(wide, lax.rem(blk + d, nb)) for d in range(1, nb)]
    for peer in peers:
        pl.semaphore_signal(barrier, inc=1, device_id=peer, device_id_type=MESH)
    pl.semaphore_wait(barrier, len(peers))

    def remote(src, dst, send, recv, peer):
        return pltpu.make_async_remote_copy(
            src_ref=src, dst_ref=dst, send_sem=send, recv_sem=recv,
            device_id=peer, device_id_type=MESH,
        )

    sent = []
    mine = core * half + slot * piece

    for target in targets_z:
        copy = remote(
            feat_ref.at[pl.ds(mult(mine, 16), piece)], feat_at(blk, mine, piece),
            zs.at[target], zr.at[blk], (wide, target),
        )
        copy.start()
        sent.append(copy)

    def spread(source):
        here = feat_at(source, mine, piece)
        remote(here, here, zs.at[source], zr.at[source], (wide, source)).wait_recv()
        for d in range(1, split):
            other = lax.rem(slot + d, split)
            copy = remote(
                here, here, ps.at[source, other], pr.at[source, slot],
                ((group + other) * 2 + core, blk),
            )
            copy.start()
            sent.append(copy)

    def cross(source):
        for d in range(1, split):
            other = lax.rem(slot + d, split)
            there = feat_at(source, core * half + other * piece, piece)
            remote(
                there, there, ps.at[source, other], pr.at[source, other],
                ((group + other) * 2 + core, blk),
            ).wait_recv()
        lot = feat_at(source, core * half, half)
        copy = remote(lot, lot, cs.at[source], cr.at[source], (partner, blk))
        copy.start()
        sent.append(copy)

    def arrived(source):
        lot = feat_at(source, mate_core * half, half)
        remote(lot, lot, cs.at[source], cr.at[source], (partner, blk)).wait_recv()

    def turn_weights(first, last):
        for c in range(first, last):
            turned = w_v[:, 128 * c:128 * (c + 1)].T
            at = 128 * c
            while at < 128 * (c + 1):
                block, off = at // bw, at % bw
                count = min(bw - off, 128 * (c + 1) - at)
                to = (block // 2) * bw + off
                wt[block % 2, to:to + count, :] = turned[at - 128 * c:at - 128 * c + count]
                at += count

    def turn_targets(i):
        p = pair_at(i)
        first = mult(p * 2 * rows, 2 * rows)
        tt[p] = t_v[pl.ds(first, 2 * rows), :].T

    tiles = width // 128
    loads[1].wait()
    turn_weights(0, tiles // 3)
    spread(sources[0])
    turn_weights(tiles // 3, tiles // 2)
    for source in sources[1:]:
        spread(source)
    cross(sources[0])
    turn_weights(tiles // 2, tiles)
    for source in sources[1:]:
        cross(source)
    loads[2].wait()
    for i in range(pairs):
        turn_targets(i)
    loads[0].wait()

    step = min(512, labels)

    def errors(i):
        p = pair_at(i)
        for first in range(0, labels, step):
            scores = lax.dot_general(
                w_v[first:first + step], feat[p], (((1,), (1,)), ((), ())),
                preferred_element_type=F32,
            )
            chance = 0.5 * jnp.tanh(0.5 * scores) + 0.5
            err[p, first:first + step] = (
                chance - tt[p, first:first + step].astype(F32)
            ).astype(BF16)

    def back(p, which):
        return jnp.dot(wt[which], err[p], preferred_element_type=F32)

    def pair_copy(p):
        return remote(a_send.at[p], a_recv.at[p], as_.at[p], ar.at[p], (partner, blk))

    def first_half(i):
        p = pair_at(i)
        a_send[p] = back(p, mate_core).astype(BF16)
        copy = pair_copy(p)
        copy.start()
        sent.append(copy)

    def second_half(i):
        p = pair_at(i)
        mine_part = back(p, core)
        for n in range(2):
            part[p * 2 + n] = mine_part[:, n * rows:(n + 1) * rows].reshape(chips, bw, rows)

    def blocks_of(i):
        return [mate, blk] if i == 0 else [pair_at(i) * 2, pair_at(i) * 2 + 1]

    def to_chips(i):
        p = pair_at(i)
        pair_copy(p).wait_recv()
        for n in range(2):
            theirs = a_recv[p, :, n * rows:(n + 1) * rows].astype(F32)
            total = part[p * 2 + n] + theirs.reshape(chips, bw, rows)
            part[p * 2 + n] = total
            b_send[p * 2 + n] = total.astype(BF16)
        for q in blocks_of(i):
            for d in range(1, chips):
                other = lax.rem(chip + d, chips)
                copy = remote(
                    b_send.at[q, other], b_recv.at[q, chip], bs.at[q, other], br.at[q, chip],
                    (other * 2 + core, blk),
                )
                copy.start()
                sent.append(copy)

    def block_sum(q):
        total = part[q, chip]
        for d in range(1, chips):
            other = lax.rem(chip + d, chips)
            remote(
                b_send.at[q, other], b_recv.at[q, other], bs.at[q, other], br.at[q, other],
                (other * 2 + core, blk),
            ).wait_recv()
            total = total + b_recv[q, other].astype(F32)
        return total

    def to_blocks(i):
        for q in [mate] if i == 0 else blocks_of(i):
            c_send[q] = block_sum(q).astype(BF16)
            copy = remote(c_send.at[q], c_recv.at[blk], xs.at[q], xr.at[blk], (wide, q))
            copy.start()
            sent.append(copy)

    chunk = min(256, labels)

    def update(n):
        first = n * chunk
        span = slice(first, first + chunk)
        grad = jnp.dot(err[0, span], feat[0], preferred_element_type=F32)
        for p in range(1, pairs):
            grad = grad + jnp.dot(err[p, span], feat[p], preferred_element_type=F32)
        moment = (0.9 * m_v[span].astype(F32) + grad).astype(BF16)
        om_v[span] = moment
        ow_v[span] = (w_v[span].astype(F32) - 0.002 * moment.astype(F32)).astype(BF16)

    updates = list(range(labels // chunk))

    def some_updates(count):
        for n in updates[:count]:
            update(n)
        del updates[:count]

    arrived(sources[0])
    errors(0)
    first_half(0)
    second_half(0)
    for i in range(1, pairs):
        arrived(sources[2 * i - 1])
        arrived(sources[2 * i])
        to_chips(i - 1)
        errors(i)
        first_half(i)
        second_half(i)
        if i >= 2:
            to_blocks(i - 2)
    to_chips(pairs - 1)
    loads[3].wait()
    some_updates(1)
    if pairs >= 2:
        to_blocks(pairs - 2)
    some_updates(2)
    to_blocks(pairs - 1)
    some_updates(len(updates))

    total = block_sum(blk)
    for d in range(1, nb):
        other = lax.rem(blk + d, nb)
        remote(
            c_send.at[other], c_recv.at[other], xs.at[other], xr.at[other], (wide, other)
        ).wait_recv()
        total = total + c_recv[other].astype(F32)
    fg_ref[...] = total.astype(BF16)

    for copy in sent:
        copy.wait_send()


def keep(w_ref, m_ref, g_ref, w_out, m_out, g_out, sems):
    count = w_ref.shape[0] // parts
    copies = [pltpu.make_async_copy(g_ref, g_out, sems.at[2 * parts])]
    for n in range(parts):
        span = pl.ds(n * count, count)
        copies.append(pltpu.make_async_copy(w_ref.at[span], w_out.at[span], sems.at[2 * n]))
        copies.append(pltpu.make_async_copy(m_ref.at[span], m_out.at[span], sems.at[2 * n + 1]))
    for copy in copies:
        copy.start()
    for copy in copies:
        copy.wait()


def solution(mesh):
    nw, nb = mesh.shape["wide"], mesh.shape["blk"]
    chips = nw // 2

    def shards(features, weights, momentum, targets):
        rows, width = features.shape
        labels = weights.shape[0]
        split = chips
        while split > 1 and (chips % split or rows % (32 * split)):
            split -= 1
        bw = width // nw
        pairs = nb // 2
        total_rows = targets.shape[0]
        flops = 6 * total_rows * labels * width
        hbm = pl.BlockSpec(memory_space=pl.ANY)
        vmem = pl.BlockSpec(memory_space=pltpu.VMEM)
        dma = pltpu.SemaphoreType.DMA
        new_weights, new_momentum, feature_grad = pl.pallas_call(
            functools.partial(kernel, nw, nb, split),
            out_shape=(
                pltpu.VMEM(weights.shape, BF16),
                pltpu.VMEM(momentum.shape, BF16),
                pltpu.VMEM((bw, rows), BF16),
            ),
            in_specs=[hbm, hbm, hbm, hbm],
            out_specs=(vmem, vmem, vmem),
            scratch_shapes=[
                pltpu.VMEM((pairs, 2 * rows, width), BF16),
                pltpu.VMEM((labels, width), BF16),
                pltpu.VMEM((labels, width), BF16),
                pltpu.VMEM((total_rows, labels), BF16),
                pltpu.VMEM((pairs, labels, 2 * rows), BF16),
                pltpu.VMEM((2, width // 2, labels), BF16),
                pltpu.VMEM((pairs, labels, 2 * rows), BF16),
                pltpu.VMEM((pairs, width // 2, 2 * rows), BF16),
                pltpu.VMEM((pairs, width // 2, 2 * rows), BF16),
                pltpu.VMEM((nb, chips, bw, rows), F32),
                pltpu.VMEM((nb, chips, bw, rows), BF16),
                pltpu.VMEM((nb, chips, bw, rows), BF16),
                pltpu.VMEM((nb, bw, rows), BF16),
                pltpu.VMEM((nb, bw, rows), BF16),
                dma((4,)),
                dma((nb,)), dma((nb,)),
                dma((nb, split)), dma((nb, split)),
                dma((nb,)), dma((nb,)),
                dma((pairs,)), dma((pairs,)),
                dma((nb, chips)), dma((nb, chips)),
                dma((nb,)), dma((nb,)),
            ],
            compiler_params=pltpu.CompilerParams(
                collective_id=0, has_side_effects=True, vmem_limit_bytes=56 * 1024 * 1024
            ),
            cost_estimate=pl.CostEstimate(
                flops=flops, bytes_accessed=8 * labels * width, transcendentals=total_rows * labels
            ),
        )(features, weights, momentum, targets)
        new_weights, new_momentum, feature_grad = pl.pallas_call(
            keep,
            out_shape=tuple(
                jax.ShapeDtypeStruct(shape, BF16) for shape in (weights.shape, momentum.shape, (bw, rows))
            ),
            in_specs=[vmem] * 3,
            out_specs=(hbm,) * 3,
            scratch_shapes=[dma((2 * parts + 1,))],
            compiler_params=pltpu.CompilerParams(vmem_limit_bytes=48 * 1024 * 1024),
        )(new_weights, new_momentum, feature_grad)
        return new_weights, new_momentum, feature_grad.T

    placed = (
        P("blk", None),
        P(("wide", "blk"), None),
        P(("wide", "blk"), None),
        P(None, ("wide", "blk")),
    )
    return jax.shard_map(
        shards,
        mesh=mesh,
        in_specs=placed,
        out_specs=(P(("wide", "blk"), None), P(("wide", "blk"), None), P("blk", "wide")),
        check_vma=False,
    )
```

```python
import functools

import jax
import jax.numpy as jnp
from jax import lax
from jax.experimental import pallas as pl
from jax.experimental.pallas import tpu as pltpu
from jax.sharding import PartitionSpec as P

F32 = jnp.float32
BF16 = jnp.bfloat16
MESH = pl.DeviceIdType.MESH
parts = 4


def mult(value, by):
    return value if isinstance(value, int) else pl.multiple_of(value, by)


def kernel(
    nw, nb, split,
    feat_ref, w_hbm, m_hbm, t_hbm,
    ow_v, om_v, fg_ref,
    feat, w_v, m_v, t_v, tt, wt, err,
    a_send, a_recv, part, b_send, b_recv, c_send, c_recv,
    load_sem, zs, zr, ps, pr, cs, cr, as_, ar, bs, br, xs, xr,
):
    rows = feat_ref.shape[0]
    labels, width = w_hbm.shape
    chips = nw // 2
    bw = width // nw
    pairs = nb // 2
    half = rows // 2
    piece = half // split

    wide = lax.axis_index("wide")
    blk = lax.axis_index("blk")
    core = lax.rem(wide, 2)
    chip = lax.div(wide, 2)
    mate_core = 1 - core
    partner = chip * 2 + mate_core
    slot = lax.rem(chip, split)
    group = chip - slot
    pair = lax.div(blk, 2)
    mate = pair * 2 + 1 - lax.rem(blk, 2)

    def pair_at(i):
        return lax.rem(pair + i, pairs)

    sources = [mate]
    for i in range(1, pairs):
        sources += [pair_at(i) * 2, pair_at(i) * 2 + 1]
    targets_z = [mate]
    for i in range(1, pairs):
        back = lax.rem(pair - i + pairs, pairs)
        targets_z += [back * 2, back * 2 + 1]

    def feat_at(block, first, count):
        start = lax.rem(block, 2) * rows + first
        return feat.at[lax.div(block, 2), pl.ds(mult(start, 16), count)]

    loads = [
        pltpu.make_async_copy(feat_ref, feat_at(blk, 0, rows), load_sem.at[0]),
        pltpu.make_async_copy(w_hbm, w_v, load_sem.at[1]),
        pltpu.make_async_copy(t_hbm, t_v, load_sem.at[2]),
        pltpu.make_async_copy(m_hbm, m_v, load_sem.at[3]),
    ]
    for load in loads:
        load.start()

    barrier = pltpu.get_barrier_semaphore()
    peers = [(partner, blk)]
    peers += [(lax.rem(chip + d, chips) * 2 + core, blk) for d in range(1, chips)]
    peers += [(wide, lax.rem(blk + d, nb)) for d in range(1, nb)]
    for peer in peers:
        pl.semaphore_signal(barrier, inc=1, device_id=peer, device_id_type=MESH)
    pl.semaphore_wait(barrier, len(peers))

    def remote(src, dst, send, recv, peer):
        return pltpu.make_async_remote_copy(
            src_ref=src, dst_ref=dst, send_sem=send, recv_sem=recv,
            device_id=peer, device_id_type=MESH,
        )

    sent = []
    mine = core * half + slot * piece

    for target in targets_z[1:] + [mate]:
        first, count = (core * half, half) if target is mate else (mine, piece)
        copy = remote(
            feat_ref.at[pl.ds(mult(first, 16), count)], feat_at(blk, first, count),
            zs.at[target], zr.at[blk], (wide, target),
        )
        copy.start()
        sent.append(copy)

    def spread(source):
        here = feat_at(source, mine, piece)
        remote(here, here, zs.at[source], zr.at[source], (wide, source)).wait_recv()
        for d in range(1, split):
            other = lax.rem(slot + d, split)
            copy = remote(
                here, here, ps.at[source, other], pr.at[source, slot],
                ((group + other) * 2 + core, blk),
            )
            copy.start()
            sent.append(copy)

    def cross(source):
        if source is mate:
            whole = feat_at(source, core * half, half)
            remote(whole, whole, zs.at[source], zr.at[source], (wide, source)).wait_recv()
        for d in range(1, 1 if source is mate else split):
            other = lax.rem(slot + d, split)
            there = feat_at(source, core * half + other * piece, piece)
            remote(
                there, there, ps.at[source, other], pr.at[source, other],
                ((group + other) * 2 + core, blk),
            ).wait_recv()
        lot = feat_at(source, core * half, half)
        copy = remote(lot, lot, cs.at[source], cr.at[source], (partner, blk))
        copy.start()
        sent.append(copy)

    def arrived(source):
        lot = feat_at(source, mate_core * half, half)
        remote(lot, lot, cs.at[source], cr.at[source], (partner, blk)).wait_recv()

    def turn_weights(first, last):
        for c in range(first, last):
            turned = w_v[:, 128 * c:128 * (c + 1)].T
            at = 128 * c
            while at < 128 * (c + 1):
                block, off = at // bw, at % bw
                count = min(bw - off, 128 * (c + 1) - at)
                to = (block // 2) * bw + off
                wt[block % 2, to:to + count, :] = turned[at - 128 * c:at - 128 * c + count]
                at += count

    def turn_targets(i):
        p = pair_at(i)
        first = mult(p * 2 * rows, 2 * rows)
        tt[p] = t_v[pl.ds(first, 2 * rows), :].T

    tiles = width // 128
    loads[1].wait()
    turn_weights(0, tiles // 3)
    for source in sources[1:]:
        spread(source)
    turn_weights(tiles // 3, tiles // 2)
    cross(mate)
    loads[2].wait()
    turn_targets(0)
    turn_weights(tiles // 2, tiles)
    loads[0].wait()

    step = min(512, labels)

    def errors(i):
        p = pair_at(i)
        for first in range(0, labels, step):
            scores = lax.dot_general(
                w_v[first:first + step], feat[p], (((1,), (1,)), ((), ())),
                preferred_element_type=F32,
            )
            chance = 0.5 * jnp.tanh(0.5 * scores) + 0.5
            err[p, first:first + step] = (
                chance - tt[p, first:first + step].astype(F32)
            ).astype(BF16)

    def back(p, which):
        return jnp.dot(wt[which], err[p], preferred_element_type=F32)

    def pair_copy(p):
        return remote(a_send.at[p], a_recv.at[p], as_.at[p], ar.at[p], (partner, blk))

    def first_half(i):
        p = pair_at(i)
        a_send[p] = back(p, mate_core).astype(BF16)
        copy = pair_copy(p)
        copy.start()
        sent.append(copy)

    def second_half(i):
        p = pair_at(i)
        mine_part = back(p, core)
        for n in range(2):
            part[p * 2 + n] = mine_part[:, n * rows:(n + 1) * rows].reshape(chips, bw, rows)

    def blocks_of(i):
        return [mate, blk] if i == 0 else [pair_at(i) * 2, pair_at(i) * 2 + 1]

    def to_chips(i):
        p = pair_at(i)
        pair_copy(p).wait_recv()
        for n in range(2):
            theirs = a_recv[p, :, n * rows:(n + 1) * rows].astype(F32)
            total = part[p * 2 + n] + theirs.reshape(chips, bw, rows)
            part[p * 2 + n] = total
            b_send[p * 2 + n] = total.astype(BF16)
        for q in blocks_of(i):
            for d in range(1, chips):
                other = lax.rem(chip + d, chips)
                copy = remote(
                    b_send.at[q, other], b_recv.at[q, chip], bs.at[q, other], br.at[q, chip],
                    (other * 2 + core, blk),
                )
                copy.start()
                sent.append(copy)

    def block_sum(q):
        total = part[q, chip]
        for d in range(1, chips):
            other = lax.rem(chip + d, chips)
            remote(
                b_send.at[q, other], b_recv.at[q, other], bs.at[q, other], br.at[q, other],
                (other * 2 + core, blk),
            ).wait_recv()
            total = total + b_recv[q, other].astype(F32)
        return total

    def to_blocks(i):
        for q in [mate] if i == 0 else blocks_of(i):
            c_send[q] = block_sum(q).astype(BF16)
            copy = remote(c_send.at[q], c_recv.at[blk], xs.at[q], xr.at[blk], (wide, q))
            copy.start()
            sent.append(copy)

    chunk = min(256, labels)

    def update(n):
        first = n * chunk
        span = slice(first, first + chunk)
        grad = jnp.dot(err[0, span], feat[0], preferred_element_type=F32)
        for p in range(1, pairs):
            grad = grad + jnp.dot(err[p, span], feat[p], preferred_element_type=F32)
        moment = (0.9 * m_v[span].astype(F32) + grad).astype(BF16)
        om_v[span] = moment
        ow_v[span] = (w_v[span].astype(F32) - 0.002 * moment.astype(F32)).astype(BF16)

    updates = list(range(labels // chunk))

    def some_updates(count):
        for n in updates[:count]:
            update(n)
        del updates[:count]

    arrived(sources[0])
    errors(0)
    for source in sources[1:]:
        cross(source)
    first_half(0)
    second_half(0)
    for i in range(1, pairs):
        turn_targets(i)
    for i in range(1, pairs):
        arrived(sources[2 * i - 1])
        arrived(sources[2 * i])
        to_chips(i - 1)
        errors(i)
        first_half(i)
        second_half(i)
        if i >= 2:
            to_blocks(i - 2)
    to_chips(pairs - 1)
    loads[3].wait()
    some_updates(1)
    if pairs >= 2:
        to_blocks(pairs - 2)
    some_updates(2)
    to_blocks(pairs - 1)
    some_updates(len(updates))

    total = block_sum(blk)
    for d in range(1, nb):
        other = lax.rem(blk + d, nb)
        remote(
            c_send.at[other], c_recv.at[other], xs.at[other], xr.at[other], (wide, other)
        ).wait_recv()
        total = total + c_recv[other].astype(F32)
    fg_ref[...] = total.astype(BF16)

    for copy in sent:
        copy.wait_send()


def keep(w_ref, m_ref, g_ref, w_out, m_out, g_out, sems):
    count = w_ref.shape[0] // parts
    copies = [pltpu.make_async_copy(g_ref, g_out, sems.at[2 * parts])]
    for n in range(parts):
        span = pl.ds(n * count, count)
        copies.append(pltpu.make_async_copy(w_ref.at[span], w_out.at[span], sems.at[2 * n]))
        copies.append(pltpu.make_async_copy(m_ref.at[span], m_out.at[span], sems.at[2 * n + 1]))
    for copy in copies:
        copy.start()
    for copy in copies:
        copy.wait()


def solution(mesh):
    nw, nb = mesh.shape["wide"], mesh.shape["blk"]
    chips = nw // 2

    def shards(features, weights, momentum, targets):
        rows, width = features.shape
        labels = weights.shape[0]
        split = chips
        while split > 1 and (chips % split or rows % (32 * split)):
            split -= 1
        bw = width // nw
        pairs = nb // 2
        total_rows = targets.shape[0]
        flops = 6 * total_rows * labels * width
        hbm = pl.BlockSpec(memory_space=pl.ANY)
        vmem = pl.BlockSpec(memory_space=pltpu.VMEM)
        dma = pltpu.SemaphoreType.DMA
        new_weights, new_momentum, feature_grad = pl.pallas_call(
            functools.partial(kernel, nw, nb, split),
            out_shape=(
                pltpu.VMEM(weights.shape, BF16),
                pltpu.VMEM(momentum.shape, BF16),
                pltpu.VMEM((bw, rows), BF16),
            ),
            in_specs=[hbm, hbm, hbm, hbm],
            out_specs=(vmem, vmem, vmem),
            scratch_shapes=[
                pltpu.VMEM((pairs, 2 * rows, width), BF16),
                pltpu.VMEM((labels, width), BF16),
                pltpu.VMEM((labels, width), BF16),
                pltpu.VMEM((total_rows, labels), BF16),
                pltpu.VMEM((pairs, labels, 2 * rows), BF16),
                pltpu.VMEM((2, width // 2, labels), BF16),
                pltpu.VMEM((pairs, labels, 2 * rows), BF16),
                pltpu.VMEM((pairs, width // 2, 2 * rows), BF16),
                pltpu.VMEM((pairs, width // 2, 2 * rows), BF16),
                pltpu.VMEM((nb, chips, bw, rows), F32),
                pltpu.VMEM((nb, chips, bw, rows), BF16),
                pltpu.VMEM((nb, chips, bw, rows), BF16),
                pltpu.VMEM((nb, bw, rows), BF16),
                pltpu.VMEM((nb, bw, rows), BF16),
                dma((4,)),
                dma((nb,)), dma((nb,)),
                dma((nb, split)), dma((nb, split)),
                dma((nb,)), dma((nb,)),
                dma((pairs,)), dma((pairs,)),
                dma((nb, chips)), dma((nb, chips)),
                dma((nb,)), dma((nb,)),
            ],
            compiler_params=pltpu.CompilerParams(
                collective_id=0, has_side_effects=True, vmem_limit_bytes=56 * 1024 * 1024
            ),
            cost_estimate=pl.CostEstimate(
                flops=flops, bytes_accessed=8 * labels * width, transcendentals=total_rows * labels
            ),
        )(features, weights, momentum, targets)
        new_weights, new_momentum, feature_grad = pl.pallas_call(
            keep,
            out_shape=tuple(
                jax.ShapeDtypeStruct(shape, BF16) for shape in (weights.shape, momentum.shape, (bw, rows))
            ),
            in_specs=[vmem] * 3,
            out_specs=(hbm,) * 3,
            scratch_shapes=[dma((2 * parts + 1,))],
            compiler_params=pltpu.CompilerParams(vmem_limit_bytes=48 * 1024 * 1024),
        )(new_weights, new_momentum, feature_grad)
        return new_weights, new_momentum, feature_grad.T

    placed = (
        P("blk", None),
        P(("wide", "blk"), None),
        P(("wide", "blk"), None),
        P(None, ("wide", "blk")),
    )
    return jax.shard_map(
        shards,
        mesh=mesh,
        in_specs=placed,
        out_specs=(P(("wide", "blk"), None), P(("wide", "blk"), None), P("blk", "wide")),
        check_vma=False,
    )
```

```python
import functools

import jax
import jax.numpy as jnp
from jax import lax
from jax.experimental import pallas as pl
from jax.experimental.pallas import tpu as pltpu
from jax.sharding import PartitionSpec as P

F32 = jnp.float32
BF16 = jnp.bfloat16
MESH = pl.DeviceIdType.MESH
parts = 4


def mult(value, by):
    return value if isinstance(value, int) else pl.multiple_of(value, by)


def others(me, count):
    if count & (count - 1):
        return [lax.rem(me + d, count) for d in range(1, count)]
    found = []
    for mask in range(count - 1, 0, -1):
        other, bit = 0, 1
        while bit < count:
            mine = lax.rem(lax.div(me, bit), 2)
            other = other + bit * (1 - mine if mask & bit else mine)
            bit *= 2
        found.append(other)
    return found


def kernel(
    nw, nb, split,
    feat_ref, w_hbm, m_hbm, t_hbm,
    ow_v, om_v, fg_ref,
    feat, w_v, m_v, t_v, tt, wt, err,
    a_send, a_recv, part, b_send, b_recv, c_send, c_recv,
    load_sem, zs, zr, ps, pr, cs, cr, as_, ar, bs, br, xs, xr,
):
    rows = feat_ref.shape[0]
    labels, width = w_hbm.shape
    chips = nw // 2
    bw = width // nw
    pairs = nb // 2
    half = rows // 2
    piece = half // split

    wide = lax.axis_index("wide")
    blk = lax.axis_index("blk")
    core = lax.rem(wide, 2)
    chip = lax.div(wide, 2)
    mate_core = 1 - core
    partner = chip * 2 + mate_core
    slot = lax.rem(chip, split)
    group = chip - slot
    pair = lax.div(blk, 2)
    mate = pair * 2 + 1 - lax.rem(blk, 2)

    def pair_at(i):
        return lax.rem(pair + i, pairs)

    sources = [mate]
    for i in range(1, pairs):
        sources += [pair_at(i) * 2, pair_at(i) * 2 + 1]
    targets_z = [mate]
    for i in range(1, pairs):
        back = lax.rem(pair - i + pairs, pairs)
        targets_z += [back * 2, back * 2 + 1]

    def feat_at(block, first, count):
        start = lax.rem(block, 2) * rows + first
        return feat.at[lax.div(block, 2), pl.ds(mult(start, 16), count)]

    loads = [
        pltpu.make_async_copy(feat_ref, feat_at(blk, 0, rows), load_sem.at[0]),
        pltpu.make_async_copy(w_hbm, w_v, load_sem.at[1]),
        pltpu.make_async_copy(t_hbm, t_v, load_sem.at[2]),
        pltpu.make_async_copy(m_hbm, m_v, load_sem.at[3]),
    ]
    for load in loads:
        load.start()

    barrier = pltpu.get_barrier_semaphore()
    peers = [(partner, blk)]
    peers += [(lax.rem(chip + d, chips) * 2 + core, blk) for d in range(1, chips)]
    peers += [(wide, lax.rem(blk + d, nb)) for d in range(1, nb)]
    for peer in peers:
        pl.semaphore_signal(barrier, inc=1, device_id=peer, device_id_type=MESH)
    pl.semaphore_wait(barrier, len(peers))

    def remote(src, dst, send, recv, peer):
        return pltpu.make_async_remote_copy(
            src_ref=src, dst_ref=dst, send_sem=send, recv_sem=recv,
            device_id=peer, device_id_type=MESH,
        )

    sent = []
    mine = core * half + slot * piece

    for target in targets_z[1:] + [mate]:
        first, count = (core * half, half) if target is mate else (mine, piece)
        copy = remote(
            feat_ref.at[pl.ds(mult(first, 16), count)], feat_at(blk, first, count),
            zs.at[target], zr.at[blk], (wide, target),
        )
        copy.start()
        sent.append(copy)

    def spread(source):
        here = feat_at(source, mine, piece)
        remote(here, here, zs.at[source], zr.at[source], (wide, source)).wait_recv()
        for other in others(slot, split):
            copy = remote(
                here, here, ps.at[source, other], pr.at[source, slot],
                ((group + other) * 2 + core, blk),
            )
            copy.start()
            sent.append(copy)

    def cross(source):
        if source is mate:
            whole = feat_at(source, core * half, half)
            remote(whole, whole, zs.at[source], zr.at[source], (wide, source)).wait_recv()
        for other in [] if source is mate else others(slot, split):
            there = feat_at(source, core * half + other * piece, piece)
            remote(
                there, there, ps.at[source, other], pr.at[source, other],
                ((group + other) * 2 + core, blk),
            ).wait_recv()
        lot = feat_at(source, core * half, half)
        copy = remote(lot, lot, cs.at[source], cr.at[source], (partner, blk))
        copy.start()
        sent.append(copy)

    def arrived(source):
        lot = feat_at(source, mate_core * half, half)
        remote(lot, lot, cs.at[source], cr.at[source], (partner, blk)).wait_recv()

    def turn_weights(first, last):
        for c in range(first, last):
            turned = w_v[:, 128 * c:128 * (c + 1)].T
            at = 128 * c
            while at < 128 * (c + 1):
                block, off = at // bw, at % bw
                count = min(bw - off, 128 * (c + 1) - at)
                to = (block // 2) * bw + off
                wt[block % 2, to:to + count, :] = turned[at - 128 * c:at - 128 * c + count]
                at += count

    def turn_targets(i):
        p = pair_at(i)
        first = mult(p * 2 * rows, 2 * rows)
        tt[p] = t_v[pl.ds(first, 2 * rows), :].T

    tiles = width // 128
    order = list(range(1, pairs)) + [0]
    loads[1].wait()
    turn_weights(0, tiles // 3)
    for source in sources[1:]:
        spread(source)
    turn_weights(tiles // 3, tiles // 2)
    loads[2].wait()
    turn_targets(order[0])
    cross(mate)
    turn_weights(tiles // 2, tiles)
    for source in sources[1:]:
        cross(source)
    loads[0].wait()

    step = min(512, labels)

    def errors(i):
        p = pair_at(i)
        for first in range(0, labels, step):
            scores = lax.dot_general(
                w_v[first:first + step], feat[p], (((1,), (1,)), ((), ())),
                preferred_element_type=F32,
            )
            chance = 0.5 * jnp.tanh(0.5 * scores) + 0.5
            err[p, first:first + step] = (
                chance - tt[p, first:first + step].astype(F32)
            ).astype(BF16)

    def back(p, which):
        return jnp.dot(wt[which], err[p], preferred_element_type=F32)

    def pair_copy(p):
        return remote(a_send.at[p], a_recv.at[p], as_.at[p], ar.at[p], (partner, blk))

    def first_half(i):
        p = pair_at(i)
        a_send[p] = back(p, mate_core).astype(BF16)
        copy = pair_copy(p)
        copy.start()
        sent.append(copy)

    def second_half(i):
        p = pair_at(i)
        mine_part = back(p, core)
        for n in range(2):
            part[p * 2 + n] = mine_part[:, n * rows:(n + 1) * rows].reshape(chips, bw, rows)

    def blocks_of(i):
        return [mate, blk] if i == 0 else [pair_at(i) * 2, pair_at(i) * 2 + 1]

    def to_chips(i):
        p = pair_at(i)
        pair_copy(p).wait_recv()
        for n in range(2):
            theirs = a_recv[p, :, n * rows:(n + 1) * rows].astype(F32)
            total = part[p * 2 + n] + theirs.reshape(chips, bw, rows)
            part[p * 2 + n] = total
            b_send[p * 2 + n] = total.astype(BF16)
        for q in blocks_of(i):
            for other in others(chip, chips):
                copy = remote(
                    b_send.at[q, other], b_recv.at[q, chip], bs.at[q, other], br.at[q, chip],
                    (other * 2 + core, blk),
                )
                copy.start()
                sent.append(copy)

    def block_sum(q):
        total = part[q, chip]
        for other in others(chip, chips):
            remote(
                b_send.at[q, other], b_recv.at[q, other], bs.at[q, other], br.at[q, other],
                (other * 2 + core, blk),
            ).wait_recv()
            total = total + b_recv[q, other].astype(F32)
        return total

    def to_blocks(i):
        for q in [mate] if i == 0 else blocks_of(i):
            c_send[q] = block_sum(q).astype(BF16)
            copy = remote(c_send.at[q], c_recv.at[blk], xs.at[q], xr.at[blk], (wide, q))
            copy.start()
            sent.append(copy)

    chunk = min(256, labels)

    def update(n):
        first = n * chunk
        span = slice(first, first + chunk)
        grad = jnp.dot(err[0, span], feat[0], preferred_element_type=F32)
        for p in range(1, pairs):
            grad = grad + jnp.dot(err[p, span], feat[p], preferred_element_type=F32)
        moment = (0.9 * m_v[span].astype(F32) + grad).astype(BF16)
        om_v[span] = moment
        ow_v[span] = (w_v[span].astype(F32) - 0.002 * moment.astype(F32)).astype(BF16)

    updates = list(range(labels // chunk))

    def some_updates(count):
        for n in updates[:count]:
            update(n)
        del updates[:count]

    for at, i in enumerate(order):
        for source in [mate] if i == 0 else sources[2 * i - 1:2 * i + 1]:
            arrived(source)
        if at >= 1:
            to_chips(order[at - 1])
        errors(i)
        first_half(i)
        second_half(i)
        if at >= 2:
            to_blocks(order[at - 2])
        if at + 1 < pairs:
            turn_targets(order[at + 1])
    to_chips(order[-1])
    loads[3].wait()
    some_updates(1)
    if pairs >= 2:
        to_blocks(order[-2])
    some_updates(2)
    to_blocks(order[-1])
    some_updates(len(updates))

    total = block_sum(blk)
    for d in range(1, nb):
        other = lax.rem(blk + d, nb)
        remote(
            c_send.at[other], c_recv.at[other], xs.at[other], xr.at[other], (wide, other)
        ).wait_recv()
        total = total + c_recv[other].astype(F32)
    fg_ref[...] = total.astype(BF16)

    for copy in sent:
        copy.wait_send()


def keep(w_ref, m_ref, g_ref, w_out, m_out, g_out, sems):
    count = w_ref.shape[0] // parts
    copies = [pltpu.make_async_copy(g_ref, g_out, sems.at[2 * parts])]
    for n in range(parts):
        span = pl.ds(n * count, count)
        copies.append(pltpu.make_async_copy(w_ref.at[span], w_out.at[span], sems.at[2 * n]))
        copies.append(pltpu.make_async_copy(m_ref.at[span], m_out.at[span], sems.at[2 * n + 1]))
    for copy in copies:
        copy.start()
    for copy in copies:
        copy.wait()


def solution(mesh):
    nw, nb = mesh.shape["wide"], mesh.shape["blk"]
    chips = nw // 2

    def shards(features, weights, momentum, targets):
        rows, width = features.shape
        labels = weights.shape[0]
        split = chips
        while split > 1 and (chips % split or rows % (32 * split)):
            split -= 1
        bw = width // nw
        pairs = nb // 2
        total_rows = targets.shape[0]
        flops = 6 * total_rows * labels * width
        hbm = pl.BlockSpec(memory_space=pl.ANY)
        vmem = pl.BlockSpec(memory_space=pltpu.VMEM)
        dma = pltpu.SemaphoreType.DMA
        new_weights, new_momentum, feature_grad = pl.pallas_call(
            functools.partial(kernel, nw, nb, split),
            out_shape=(
                pltpu.VMEM(weights.shape, BF16),
                pltpu.VMEM(momentum.shape, BF16),
                pltpu.VMEM((bw, rows), BF16),
            ),
            in_specs=[hbm, hbm, hbm, hbm],
            out_specs=(vmem, vmem, vmem),
            scratch_shapes=[
                pltpu.VMEM((pairs, 2 * rows, width), BF16),
                pltpu.VMEM((labels, width), BF16),
                pltpu.VMEM((labels, width), BF16),
                pltpu.VMEM((total_rows, labels), BF16),
                pltpu.VMEM((pairs, labels, 2 * rows), BF16),
                pltpu.VMEM((2, width // 2, labels), BF16),
                pltpu.VMEM((pairs, labels, 2 * rows), BF16),
                pltpu.VMEM((pairs, width // 2, 2 * rows), BF16),
                pltpu.VMEM((pairs, width // 2, 2 * rows), BF16),
                pltpu.VMEM((nb, chips, bw, rows), F32),
                pltpu.VMEM((nb, chips, bw, rows), BF16),
                pltpu.VMEM((nb, chips, bw, rows), BF16),
                pltpu.VMEM((nb, bw, rows), BF16),
                pltpu.VMEM((nb, bw, rows), BF16),
                dma((4,)),
                dma((nb,)), dma((nb,)),
                dma((nb, split)), dma((nb, split)),
                dma((nb,)), dma((nb,)),
                dma((pairs,)), dma((pairs,)),
                dma((nb, chips)), dma((nb, chips)),
                dma((nb,)), dma((nb,)),
            ],
            compiler_params=pltpu.CompilerParams(
                collective_id=0, has_side_effects=True, vmem_limit_bytes=56 * 1024 * 1024
            ),
            cost_estimate=pl.CostEstimate(
                flops=flops, bytes_accessed=8 * labels * width, transcendentals=total_rows * labels
            ),
        )(features, weights, momentum, targets)
        new_weights, new_momentum, feature_grad = pl.pallas_call(
            keep,
            out_shape=tuple(
                jax.ShapeDtypeStruct(shape, BF16) for shape in (weights.shape, momentum.shape, (bw, rows))
            ),
            in_specs=[vmem] * 3,
            out_specs=(hbm,) * 3,
            scratch_shapes=[dma((2 * parts + 1,))],
            compiler_params=pltpu.CompilerParams(vmem_limit_bytes=48 * 1024 * 1024),
        )(new_weights, new_momentum, feature_grad)
        return new_weights, new_momentum, feature_grad.T

    placed = (
        P("blk", None),
        P(("wide", "blk"), None),
        P(("wide", "blk"), None),
        P(None, ("wide", "blk")),
    )
    return jax.shard_map(
        shards,
        mesh=mesh,
        in_specs=placed,
        out_specs=(P(("wide", "blk"), None), P(("wide", "blk"), None), P("blk", "wide")),
        check_vma=False,
    )
```

```python
import functools

import jax
import jax.numpy as jnp
from jax import lax
from jax.experimental import pallas as pl
from jax.experimental.pallas import tpu as pltpu
from jax.sharding import PartitionSpec as P

F32 = jnp.float32
BF16 = jnp.bfloat16
MESH = pl.DeviceIdType.MESH
parts = 4


def mult(value, by):
    return value if isinstance(value, int) else pl.multiple_of(value, by)


def others(me, count):
    if count & (count - 1):
        return [lax.rem(me + d, count) for d in range(1, count)]
    found = []
    for mask in range(count - 1, 0, -1):
        other, bit = 0, 1
        while bit < count:
            mine = lax.rem(lax.div(me, bit), 2)
            other = other + bit * (1 - mine if mask & bit else mine)
            bit *= 2
        found.append(other)
    return found


def kernel(
    nw, nb, split,
    feat_ref, w_hbm, m_hbm, t_hbm,
    ow_v, om_v, fg_ref,
    feat, w_v, m_v, t_v, tt, wt, err,
    a_send, a_recv, part, b_send, b_recv, c_send, c_recv,
    load_sem, zs, zr, ps, pr, cs, cr, as_, ar, bs, br, xs, xr,
):
    rows = feat_ref.shape[0]
    labels, width = w_hbm.shape
    chips = nw // 2
    bw = width // nw
    pairs = nb // 2
    half = rows // 2
    piece = half // split

    wide = lax.axis_index("wide")
    blk = lax.axis_index("blk")
    core = lax.rem(wide, 2)
    chip = lax.div(wide, 2)
    mate_core = 1 - core
    partner = chip * 2 + mate_core
    slot = lax.rem(chip, split)
    group = chip - slot
    pair = lax.div(blk, 2)
    mate = pair * 2 + 1 - lax.rem(blk, 2)

    def pair_at(i):
        return lax.rem(pair + i, pairs)

    sources = [mate]
    for i in range(1, pairs):
        sources += [pair_at(i) * 2, pair_at(i) * 2 + 1]
    targets_z = [mate]
    for i in range(1, pairs):
        back = lax.rem(pair - i + pairs, pairs)
        targets_z += [back * 2, back * 2 + 1]

    def feat_at(block, first, count):
        start = lax.rem(block, 2) * rows + first
        return feat.at[lax.div(block, 2), pl.ds(mult(start, 16), count)]

    loads = [
        pltpu.make_async_copy(feat_ref, feat_at(blk, 0, rows), load_sem.at[0]),
        pltpu.make_async_copy(w_hbm, w_v, load_sem.at[1]),
        pltpu.make_async_copy(t_hbm, t_v, load_sem.at[2]),
        pltpu.make_async_copy(m_hbm, m_v, load_sem.at[3]),
    ]
    for load in loads:
        load.start()

    barrier = pltpu.get_barrier_semaphore()
    peers = [(partner, blk)]
    peers += [(lax.rem(chip + d, chips) * 2 + core, blk) for d in range(1, chips)]
    peers += [(wide, lax.rem(blk + d, nb)) for d in range(1, nb)]
    for peer in peers:
        pl.semaphore_signal(barrier, inc=1, device_id=peer, device_id_type=MESH)
    pl.semaphore_wait(barrier, len(peers))

    def remote(src, dst, send, recv, peer):
        return pltpu.make_async_remote_copy(
            src_ref=src, dst_ref=dst, send_sem=send, recv_sem=recv,
            device_id=peer, device_id_type=MESH,
        )

    sent = []
    mine = core * half + slot * piece

    for target in targets_z[1:] + [mate]:
        first, count = (core * half, half) if target is mate else (mine, piece)
        copy = remote(
            feat_ref.at[pl.ds(mult(first, 16), count)], feat_at(blk, first, count),
            zs.at[target], zr.at[blk], (wide, target),
        )
        copy.start()
        sent.append(copy)

    def spread(source):
        here = feat_at(source, mine, piece)
        remote(here, here, zs.at[source], zr.at[source], (wide, source)).wait_recv()
        for other in others(slot, split):
            copy = remote(
                here, here, ps.at[source, other], pr.at[source, slot],
                ((group + other) * 2 + core, blk),
            )
            copy.start()
            sent.append(copy)

    def cross(source):
        if source is mate:
            whole = feat_at(source, core * half, half)
            remote(whole, whole, zs.at[source], zr.at[source], (wide, source)).wait_recv()
        for other in [] if source is mate else others(slot, split):
            there = feat_at(source, core * half + other * piece, piece)
            remote(
                there, there, ps.at[source, other], pr.at[source, other],
                ((group + other) * 2 + core, blk),
            ).wait_recv()
        lot = feat_at(source, core * half, half)
        copy = remote(lot, lot, cs.at[source], cr.at[source], (partner, blk))
        copy.start()
        sent.append(copy)

    def arrived(source):
        lot = feat_at(source, mate_core * half, half)
        remote(lot, lot, cs.at[source], cr.at[source], (partner, blk)).wait_recv()

    def turn_weights(first, last):
        for c in range(first, last):
            turned = w_v[:, 128 * c:128 * (c + 1)].T
            at = 128 * c
            while at < 128 * (c + 1):
                block, off = at // bw, at % bw
                count = min(bw - off, 128 * (c + 1) - at)
                to = (block // 2) * bw + off
                wt[block % 2, to:to + count, :] = turned[at - 128 * c:at - 128 * c + count]
                at += count

    def turn_targets(i):
        p = pair_at(i)
        first = mult(p * 2 * rows, 2 * rows)
        tt[p] = t_v[pl.ds(first, 2 * rows), :].T

    tiles = width // 128
    order = list(range(1, pairs)) + [0]
    loads[1].wait()
    turn_weights(0, tiles // 3)
    for source in sources[1:]:
        spread(source)
    turn_weights(tiles // 3, tiles // 2)
    loads[2].wait()
    turn_targets(order[0])
    cross(mate)
    turn_weights(tiles // 2, tiles)
    for source in sources[1:]:
        cross(source)
    loads[0].wait()

    step = min(512, labels)

    def errors(i):
        p = pair_at(i)
        for first in range(0, labels, step):
            scores = lax.dot_general(
                w_v[first:first + step], feat[p], (((1,), (1,)), ((), ())),
                preferred_element_type=F32,
            )
            chance = 0.5 * jnp.tanh(0.5 * scores) + 0.5
            err[p, first:first + step] = (
                chance - tt[p, first:first + step].astype(F32)
            ).astype(BF16)

    def back(p, which):
        return jnp.dot(wt[which], err[p], preferred_element_type=F32)

    def pair_copy(p):
        return remote(a_send.at[p], a_recv.at[p], as_.at[p], ar.at[p], (partner, blk))

    def first_half(i):
        p = pair_at(i)
        a_send[p] = back(p, mate_core).astype(BF16)
        copy = pair_copy(p)
        copy.start()
        sent.append(copy)

    def second_half(i):
        p = pair_at(i)
        mine_part = back(p, core)
        for n in range(2):
            part[p * 2 + n] = mine_part[:, n * rows:(n + 1) * rows].reshape(chips, bw, rows)

    def blocks_of(i):
        return [mate, blk] if i == 0 else [pair_at(i) * 2, pair_at(i) * 2 + 1]

    def to_chips(i):
        p = pair_at(i)
        pair_copy(p).wait_recv()
        for n in range(2):
            theirs = a_recv[p, :, n * rows:(n + 1) * rows].astype(F32)
            total = part[p * 2 + n] + theirs.reshape(chips, bw, rows)
            part[p * 2 + n] = total
            b_send[p * 2 + n] = total.astype(BF16)
        for q in blocks_of(i):
            for other in others(chip, chips):
                copy = remote(
                    b_send.at[q, other], b_recv.at[q, chip], bs.at[q, other], br.at[q, chip],
                    (other * 2 + core, blk),
                )
                copy.start()
                sent.append(copy)

    def block_sum(q):
        total = part[q, chip]
        for other in others(chip, chips):
            remote(
                b_send.at[q, other], b_recv.at[q, other], bs.at[q, other], br.at[q, other],
                (other * 2 + core, blk),
            ).wait_recv()
            total = total + b_recv[q, other].astype(F32)
        return total

    def to_blocks(i):
        for q in [mate] if i == 0 else blocks_of(i):
            c_send[q] = block_sum(q).astype(BF16)
            copy = remote(c_send.at[q], c_recv.at[blk], xs.at[q], xr.at[blk], (wide, q))
            copy.start()
            sent.append(copy)

    chunk = min(256, labels)

    def update(n):
        first = n * chunk
        span = slice(first, first + chunk)
        grad = jnp.dot(err[0, span], feat[0], preferred_element_type=F32)
        for p in range(1, pairs):
            grad = grad + jnp.dot(err[p, span], feat[p], preferred_element_type=F32)
        moment = (0.9 * m_v[span].astype(F32) + grad).astype(BF16)
        om_v[span] = moment
        ow_v[span] = (w_v[span].astype(F32) - 0.002 * moment.astype(F32)).astype(BF16)

    updates = list(range(labels // chunk))

    def some_updates(count):
        for n in updates[:count]:
            update(n)
        del updates[:count]

    for at, i in enumerate(order):
        for source in [mate] if i == 0 else sources[2 * i - 1:2 * i + 1]:
            arrived(source)
        if at >= 1:
            to_chips(order[at - 1])
        errors(i)
        first_half(i)
        second_half(i)
        if at >= 2:
            to_blocks(order[at - 2])
        if at + 1 < pairs:
            turn_targets(order[at + 1])
    to_chips(order[-1])
    if pairs >= 2:
        to_blocks(order[-2])
    loads[3].wait()
    some_updates(3)
    to_blocks(order[-1])
    some_updates(len(updates))

    total = block_sum(blk)
    for d in range(1, nb):
        other = lax.rem(blk + d, nb)
        remote(
            c_send.at[other], c_recv.at[other], xs.at[other], xr.at[other], (wide, other)
        ).wait_recv()
        total = total + c_recv[other].astype(F32)
    fg_ref[...] = total.astype(BF16)

    for copy in sent:
        copy.wait_send()


def keep(w_ref, m_ref, g_ref, w_out, m_out, g_out, sems):
    count = w_ref.shape[0] // parts
    copies = [pltpu.make_async_copy(g_ref, g_out, sems.at[2 * parts])]
    for n in range(parts):
        span = pl.ds(n * count, count)
        copies.append(pltpu.make_async_copy(w_ref.at[span], w_out.at[span], sems.at[2 * n]))
        copies.append(pltpu.make_async_copy(m_ref.at[span], m_out.at[span], sems.at[2 * n + 1]))
    for copy in copies:
        copy.start()
    for copy in copies:
        copy.wait()


def solution(mesh):
    nw, nb = mesh.shape["wide"], mesh.shape["blk"]
    chips = nw // 2

    def shards(features, weights, momentum, targets):
        rows, width = features.shape
        labels = weights.shape[0]
        split = chips
        while split > 1 and (chips % split or rows % (32 * split)):
            split -= 1
        bw = width // nw
        pairs = nb // 2
        total_rows = targets.shape[0]
        flops = 6 * total_rows * labels * width
        hbm = pl.BlockSpec(memory_space=pl.ANY)
        vmem = pl.BlockSpec(memory_space=pltpu.VMEM)
        dma = pltpu.SemaphoreType.DMA
        new_weights, new_momentum, feature_grad = pl.pallas_call(
            functools.partial(kernel, nw, nb, split),
            out_shape=(
                pltpu.VMEM(weights.shape, BF16),
                pltpu.VMEM(momentum.shape, BF16),
                pltpu.VMEM((bw, rows), BF16),
            ),
            in_specs=[hbm, hbm, hbm, hbm],
            out_specs=(vmem, vmem, vmem),
            scratch_shapes=[
                pltpu.VMEM((pairs, 2 * rows, width), BF16),
                pltpu.VMEM((labels, width), BF16),
                pltpu.VMEM((labels, width), BF16),
                pltpu.VMEM((total_rows, labels), BF16),
                pltpu.VMEM((pairs, labels, 2 * rows), BF16),
                pltpu.VMEM((2, width // 2, labels), BF16),
                pltpu.VMEM((pairs, labels, 2 * rows), BF16),
                pltpu.VMEM((pairs, width // 2, 2 * rows), BF16),
                pltpu.VMEM((pairs, width // 2, 2 * rows), BF16),
                pltpu.VMEM((nb, chips, bw, rows), F32),
                pltpu.VMEM((nb, chips, bw, rows), BF16),
                pltpu.VMEM((nb, chips, bw, rows), BF16),
                pltpu.VMEM((nb, bw, rows), BF16),
                pltpu.VMEM((nb, bw, rows), BF16),
                dma((4,)),
                dma((nb,)), dma((nb,)),
                dma((nb, split)), dma((nb, split)),
                dma((nb,)), dma((nb,)),
                dma((pairs,)), dma((pairs,)),
                dma((nb, chips)), dma((nb, chips)),
                dma((nb,)), dma((nb,)),
            ],
            compiler_params=pltpu.CompilerParams(
                collective_id=0, has_side_effects=True, vmem_limit_bytes=56 * 1024 * 1024
            ),
            cost_estimate=pl.CostEstimate(
                flops=flops, bytes_accessed=8 * labels * width, transcendentals=total_rows * labels
            ),
        )(features, weights, momentum, targets)
        new_weights, new_momentum, feature_grad = pl.pallas_call(
            keep,
            out_shape=tuple(
                jax.ShapeDtypeStruct(shape, BF16) for shape in (weights.shape, momentum.shape, (bw, rows))
            ),
            in_specs=[vmem] * 3,
            out_specs=(hbm,) * 3,
            scratch_shapes=[dma((2 * parts + 1,))],
            compiler_params=pltpu.CompilerParams(vmem_limit_bytes=48 * 1024 * 1024),
        )(new_weights, new_momentum, feature_grad)
        return new_weights, new_momentum, feature_grad.T

    placed = (
        P("blk", None),
        P(("wide", "blk"), None),
        P(("wide", "blk"), None),
        P(None, ("wide", "blk")),
    )
    return jax.shard_map(
        shards,
        mesh=mesh,
        in_specs=placed,
        out_specs=(P(("wide", "blk"), None), P(("wide", "blk"), None), P("blk", "wide")),
        check_vma=False,
    )
```
